32 devices in a mesh: group: 2 (over x), tile: 16 (over z, y, core).
Axes of the slice: x: 2, y: 2, z: 4, core: 2. Of those that a mesh axis runs over, the one named last changes fastest.
Arguments:
- query_tokens: bfloat16 [6144, 1536], P(('group', 'tile')), parts along dimension 0, may hold values from -6 to 6
- key_tokens: bfloat16 [6144, 1536], P(('group', 'tile')), parts along dimension 0, may hold values from -6 to 6
- value_tokens: bfloat16 [6144, 1536], P(('group', 'tile')), parts along dimension 0, may hold values from -6 to 6
- forward_out: bfloat16 [6144, 1536], P(('group', 'tile')), parts along dimension 0, may hold values from -3 to 3
- out_grad: bfloat16 [6144, 1536], P(('group', 'tile')), parts along dimension 0, may hold values from -192 to 192
- log_norm: float32 [12, 6144], P(None, ('group', 'tile')), parts along dimension 1, may hold values from 7.5 to 9
- window_ids: int32 [12, 16, 5], P(None, 'tile'), may hold values from -1 to 15, as said below
Outputs:
- grad_queries: bfloat16 [6144, 1536], P(('group', 'tile')), parts along dimension 0
- grad_keys: bfloat16 [6144, 1536], P(('group', 'tile')), parts along dimension 0
- grad_values: bfloat16 [6144, 1536], P(('group', 'tile')), parts along dimension 0
The draws below stay inside these ranges and needn't reach their ends.
There are 2 independent parts, one for each index of `group`. The reference program is written for one: setup_inputs(seed, part) draws one part's arguments, and reference() takes and returns one part's arrays. A program takes and returns all parts, laid end to end along the dimension named above; an argument that names none is the same for every part. Nothing has to cross between parts.
Inputs may be any that keep to these rules, and one draw needn't show every extreme that they name: Tiles are numbered width fastest, then height, then time, on a grid of 2 x 1 x 8. window_ids[h, i, 0] is the tile beside tile i along time; entries 1 and 2 are the tiles before and after tile i along width; entries 3 and 4 are the tiles before and after, along width, of the tile beside i along time. An entry is -1 where that tile does not exist or lies outside head h's window; each head's window has one shape, a block of tiles along time and width, clipped at the grid's border.
All inputs are finite; a program needn't handle non-finite values.
Results may differ from the reference program's by a relative error of at most 0.0075.
Values may be sent and summed in bfloat16 or wider, within the bound.
No kernel may reach another device: no remote copies, remote signals or barrier semaphores. Data moves between devices by JAX's collectives and lax.ppermute only.
A program may use at most 64 MiB of HBM per device.

```python
import math
import jax
import jax.numpy as jnp
from jax import lax

HEADS = 12
HEAD_DIM = 128
FEAT = 1536
TILE_TOK = 192
GW = 8
GH = 1
TILES = 16
TOKENS = 3072


def draw_window_ids(key, part):
    key = jax.random.fold_in(key, 7)
    tile_ids = jnp.arange(TILES, dtype=jnp.int32)
    plane_size = GH * GW
    column = tile_ids % GW
    partner = jnp.where(tile_ids < plane_size, tile_ids + plane_size, tile_ids - plane_size)
    lower_column = jnp.where(column > 0, tile_ids - 1, -1)
    upper_column = jnp.where(column < GW - 1, tile_ids + 1, -1)
    partner_lower = jnp.where(column > 0, partner - 1, -1)
    partner_upper = jnp.where(column < GW - 1, partner + 1, -1)
    flags = jax.random.randint(key, (HEADS, 2), 0, 4) < 3
    full_head = jax.random.randint(jax.random.fold_in(key, 1), (), 0, HEADS)
    chosen = jnp.arange(HEADS, dtype=jnp.int32) == full_head
    time_on = (flags[:, 0] | chosen)[:, None]
    width_on = (flags[:, 1] | chosen)[:, None]
    both_on = time_on & width_on
    empty = jnp.zeros((HEADS, TILES), jnp.int32) - 1
    slot_time = jnp.where(time_on, partner[None, :], empty)
    slot_lower = jnp.where(width_on, lower_column[None, :], empty)
    slot_upper = jnp.where(width_on, upper_column[None, :], empty)
    slot_plower = jnp.where(both_on, partner_lower[None, :], empty)
    slot_pupper = jnp.where(both_on, partner_upper[None, :], empty)
    return jnp.stack([slot_time, slot_lower, slot_upper, slot_plower, slot_pupper], axis=2).astype(jnp.int32)


def level_of(stream_key, shape, pieces, smallest, largest):
    gain, own = 1.0, jax.random.fold_in(stream_key, 6)
    for dim, parts in pieces:
        steps = jnp.exp(jax.random.uniform(jax.random.fold_in(own, dim), (parts,), jnp.float32, smallest / len(pieces), largest / len(pieces)))
        gain = gain * jnp.repeat(steps, shape[dim] // parts).reshape([-1 if axis == dim else 1 for axis in range(len(shape))])
    return gain


def bell_draw(stream_key, extent, spread, limit, cuts=(), held_as=jnp.bfloat16):
    values = jax.random.normal(stream_key, extent, jnp.float32) * spread
    if len(cuts) > 0:
        values = level_of(stream_key, extent, cuts, -0.22, 0.18) * values
    return jnp.clip(values, min=-limit, max=limit).astype(held_as)


def setup_inputs(seed: int = 0, part: int = 0) -> dict:
    streams_of = jax.random.split(jax.random.key(seed), 8)
    part_keys = jax.random.split(jax.random.fold_in(streams_of[7], part), 8)
    return {
        "query_tokens": bell_draw(part_keys[0], (TOKENS, FEAT), 1.0, 6.0, ((0, 16),)),
        "key_tokens": bell_draw(part_keys[1], (TOKENS, FEAT), 1.0, 6.0, ((0, 16),)),
        "value_tokens": bell_draw(part_keys[2], (TOKENS, FEAT), 1.0, 6.0, ((0, 16),)),
        "forward_out": bell_draw(part_keys[3], (TOKENS, FEAT), 0.5, 3.0, ((0, 16),)),
        "out_grad": bell_draw(part_keys[4], (TOKENS, FEAT), 32.0, 192.0, ((0, 16),)),
        "log_norm": jnp.clip(7.5 + 1.5 * jax.random.uniform(part_keys[5], (HEADS, TOKENS), jnp.float32) ** level_of(part_keys[5], (HEADS, TOKENS), ((1, 16),), -0.2, 0.2), 7.5, 9.0),
        "window_ids": draw_window_ids(jax.random.fold_in(streams_of[7], 71), part),
    }


def rounded(values):
    return lax.optimization_barrier(values.astype(jnp.bfloat16)).astype(jnp.float32)

def split_heads(values):
    return values.reshape(values.shape[0], HEADS, HEAD_DIM)

def pair_terms(query_heads, grad_heads, log_part, delta_part, key_heads, value_heads):
    score_scale = 1.0 / math.sqrt(HEAD_DIM)
    best = lax.Precision.HIGHEST
    scores = jnp.einsum('thd,shd->hts', query_heads, key_heads, precision=best) * score_scale
    weights = jnp.exp(scores - log_part[:, :, None])
    weights_low = rounded(weights)
    value_term = jnp.einsum('hts,thd->shd', weights_low, grad_heads, precision=best)
    grad_weights = jnp.einsum('thd,shd->hts', grad_heads, value_heads, precision=best)
    grad_scores = rounded(weights * (grad_weights - delta_part[:, :, None]))
    query_term = jnp.einsum('hts,shd->thd', grad_scores, key_heads, precision=best) * score_scale
    key_term = jnp.einsum('hts,thd->shd', grad_scores, query_heads, precision=best) * score_scale
    return (rounded(query_term), rounded(key_term), rounded(value_term))

def reference(query_tokens, key_tokens, value_tokens, forward_out, out_grad, log_norm, window_ids):
    tile_rows = TILE_TOK
    row_delta = lax.optimization_barrier(jnp.sum(split_heads(out_grad.astype(jnp.float32) * forward_out.astype(jnp.float32)), axis=2)).T

    def take_rows(source, start):
        return split_heads(lax.dynamic_slice_in_dim(source, start, tile_rows, 0).astype(jnp.float32))

    def per_tile(totals, tile_index):
        key_total, value_total = totals
        start = (tile_index * tile_rows).astype(jnp.int32)
        query_heads = take_rows(query_tokens, start)
        grad_heads = take_rows(out_grad, start)
        log_part = lax.dynamic_slice_in_dim(log_norm, start, tile_rows, 1)
        delta_part = lax.dynamic_slice_in_dim(row_delta, start, tile_rows, 1)
        head_ids = window_ids[:, tile_index, :].astype(jnp.int32)
        self_ids = jnp.zeros((HEADS, 1), jnp.int32) + tile_index.astype(jnp.int32)
        members = jnp.concatenate([self_ids, head_ids], axis=1)
        query_total = jnp.zeros((tile_rows, HEADS, HEAD_DIM), jnp.float32)
        for slot_index in range(6):
            target = jnp.max(members[:, slot_index])
            present = (members[:, slot_index] >= 0).astype(jnp.float32)[None, :, None]
            key_start = (jnp.maximum(target, 0) * tile_rows).astype(jnp.int32)
            key_heads = take_rows(key_tokens, key_start)
            value_heads = take_rows(value_tokens, key_start)
            query_term, key_term, value_term = pair_terms(query_heads, grad_heads, log_part, delta_part, key_heads, value_heads)
            query_total = query_total + query_term * present
            key_add = (key_term * present).reshape(tile_rows, FEAT)
            value_add = (value_term * present).reshape(tile_rows, FEAT)
            old_keys = lax.dynamic_slice_in_dim(key_total, key_start, tile_rows, 0)
            key_total = lax.dynamic_update_slice_in_dim(key_total, old_keys + key_add, key_start, 0)
            old_values = lax.dynamic_slice_in_dim(value_total, key_start, tile_rows, 0)
            value_total = lax.dynamic_update_slice_in_dim(value_total, old_values + value_add, key_start, 0)
        return ((key_total, value_total), query_total.reshape(tile_rows, FEAT).astype(jnp.bfloat16))
    empty = jnp.zeros((TOKENS, FEAT), jnp.float32)
    finals, query_blocks = lax.scan(per_tile, (empty, empty), jnp.arange(TILES, dtype=jnp.int32))
    key_total, value_total = finals
    return (query_blocks.reshape(TOKENS, FEAT), key_total.astype(jnp.bfloat16), value_total.astype(jnp.bfloat16))
```

```python
import functools
import math

import jax
import jax.numpy as jnp
from jax import lax
from jax.experimental import pallas as pl
from jax.experimental.pallas import tpu as pltpu
from jax.sharding import PartitionSpec as P

GRID_WIDTH = 8
ABSENT = 1e30
LOG2E = 1.4426950408889634
NT = (((1,), (1,)), ((), ()))
TN = (((0,), (0,)), ((), ()))
VMEM_LIMIT = 32 * 2**20


def dot(a, b, dims=(((1,), (0,)), ((), ()))):
    return lax.dot_general(a, b, dims, preferred_element_type=jnp.float32)


def pack_kernel(order, window, query, grad, out, log_norm, *refs, sizes):
    chunks, own_aux, send_aux = refs[: len(sizes)], refs[-2], refs[-1]
    rows = query.shape[0]
    size = query.shape[1] // log_norm.shape[0]
    ones = jnp.ones((8, size), jnp.bfloat16)
    lane = lax.broadcasted_iota(jnp.int32, (1, own_aux.shape[2] - rows), 1)

    def flag_row(head, slots):
        row = jnp.zeros(lane.shape, jnp.float32)
        for place, slot in enumerate(slots):
            if slot is not None:
                gone = jnp.where(window[head, slot] < 0, ABSENT, 0.0)
                row = jnp.where(lane == place, gone, row)
        return row

    place = 0
    for chunk, count in zip(chunks, sizes):
        for i in range(count):
            head = order[place]
            columns = pl.ds(pl.multiple_of(head * size, size), size)
            grads = grad[:, columns]
            chunk[i, 0] = query[:, columns]
            chunk[i, 1] = grads
            product = grads.astype(jnp.float32) * out[:, columns].astype(jnp.float32)
            high = product.astype(jnp.bfloat16)
            low = (product - high.astype(jnp.float32)).astype(jnp.bfloat16)
            delta = dot(ones, high, NT) + dot(ones, low, NT)
            norm = log_norm[pl.ds(head, 1), :] * LOG2E
            for aux, slots in ((own_aux, (None, 1, 2)), (send_aux, (0, 3, 4))):
                aux[place, 0:1, :rows] = norm
                aux[place, 1:2, :rows] = delta[0:1]
                aux[place, 0:1, rows:] = flag_row(head, slots)
                aux[place, 1:2, rows:] = jnp.zeros(lane.shape, jnp.float32)
            place += 1


def pack(order, window, query, grad, out, log_norm, sizes):
    rows = query.shape[0]
    heads = log_norm.shape[0]
    size = query.shape[1] // heads
    lanes = -(-(rows + 3) // 128) * 128
    whole = pl.BlockSpec(memory_space=pltpu.VMEM)
    scalar = pl.BlockSpec(memory_space=pltpu.SMEM)
    aux = jax.ShapeDtypeStruct((heads, 2, lanes), jnp.float32)
    return pl.pallas_call(
        functools.partial(pack_kernel, sizes=sizes),
        out_shape=[jax.ShapeDtypeStruct((n, 2, rows, size), jnp.bfloat16) for n in sizes] + [aux, aux],
        in_specs=[scalar, scalar] + [whole] * 4,
        out_specs=[whole] * (len(sizes) + 2),
        compiler_params=pltpu.CompilerParams(vmem_limit_bytes=VMEM_LIMIT),
        name="pack",
    )(order, window, query, grad, out, log_norm)


def terms_kernel(order, own, own_aux, other, other_aux, *refs, base, score_scale):
    keys, values, outs = refs[0:3], refs[3:6], refs[6:]
    own_query, other_query, key_values = outs[0], outs[1], outs[2:]
    rows = own.shape[2]
    place = base + pl.program_id(0)
    mine, theirs = own_aux[place], other_aux[place]
    queries = jnp.concatenate([own[0, 0], other[0, 0]], axis=0)
    grads = jnp.concatenate([own[0, 1], other[0, 1]], axis=0)
    delta = jnp.concatenate([mine[1:2, :rows], theirs[1:2, :rows]], axis=1)
    query_total = jnp.zeros(queries.shape, jnp.float32)
    for j in range(3):
        key, value = keys[j][...], values[j][...]
        norm = jnp.concatenate(
            [part[0:1, :rows] + part[0:1, rows + j : rows + j + 1] for part in (mine, theirs)], axis=1
        )
        scores = dot(key, queries, NT)
        weights = jnp.exp2(scores * (score_scale * LOG2E) - norm)
        value_term = dot(weights.astype(jnp.bfloat16), grads)
        grad_weights = dot(value, grads, NT)
        grad_scores = (weights * (grad_weights - delta)).astype(jnp.bfloat16)
        key_term = dot(grad_scores, queries) * score_scale
        query_total = query_total + dot(grad_scores, key, TN)
        key_values[j][0, 0] = key_term.astype(jnp.bfloat16)
        key_values[j][0, 1] = value_term.astype(jnp.bfloat16)
    query_total = (query_total * score_scale).astype(jnp.bfloat16)
    own_query[0] = query_total[:rows]
    other_query[0] = query_total[rows:]


def terms(order, own, own_aux, other, other_aux, keys, values, base):
    count, _, rows, size = own.shape
    score_scale = 1.0 / math.sqrt(size)
    whole = pl.BlockSpec(memory_space=pltpu.VMEM)
    packed = pl.BlockSpec((1, 2, rows, size), lambda i, order: (i, 0, 0, 0))
    one = pl.BlockSpec((1, rows, size), lambda i, order: (i, 0, 0))
    column = pl.BlockSpec((rows, size), lambda i, order: (0, order[base + i]))
    pair = jax.ShapeDtypeStruct((count, 2, rows, size), jnp.bfloat16)
    single = jax.ShapeDtypeStruct((count, rows, size), jnp.bfloat16)
    flops = count * 5 * 2 * 6 * rows * rows * size
    return pl.pallas_call(
        functools.partial(terms_kernel, base=base, score_scale=score_scale),
        out_shape=[single, single, pair, pair, pair],
        grid_spec=pltpu.PrefetchScalarGridSpec(
            num_scalar_prefetch=1,
            grid=(count,),
            in_specs=[packed, whole, packed, whole] + [column] * 6,
            out_specs=[one, one, packed, packed, packed],
        ),
        compiler_params=pltpu.CompilerParams(vmem_limit_bytes=VMEM_LIMIT),
        cost_estimate=pl.CostEstimate(
            flops=flops, bytes_accessed=count * 18 * rows * size * 2, transcendentals=count * 6 * rows * rows
        ),
        name="terms",
    )(order, own, own_aux, other, other_aux, *keys, *values)


def finish_kernel(order, *refs, sizes):
    n = len(sizes)
    own_query, back_query, own, left, right = (refs[k * n : (k + 1) * n] for k in range(5))
    query_out, key_out, value_out = refs[5 * n :]
    size = own_query[0].shape[2]
    place = 0
    for c, count in enumerate(sizes):
        for i in range(count):
            columns = pl.ds(pl.multiple_of(order[place] * size, size), size)
            query = own_query[c][i].astype(jnp.float32) + back_query[c][i].astype(jnp.float32)
            query_out[:, columns] = query.astype(jnp.bfloat16)
            for k, result in ((0, key_out), (1, value_out)):
                total = (
                    own[c][i, k].astype(jnp.float32)
                    + left[c][i, k].astype(jnp.float32)
                    + right[c][i, k].astype(jnp.float32)
                )
                result[:, columns] = total.astype(jnp.bfloat16)
            place += 1


def finish(order, parts, sizes, rows, features):
    whole = pl.BlockSpec(memory_space=pltpu.VMEM)
    result = jax.ShapeDtypeStruct((rows, features), jnp.bfloat16)
    return pl.pallas_call(
        functools.partial(finish_kernel, sizes=sizes),
        out_shape=[result] * 3,
        in_specs=[pl.BlockSpec(memory_space=pltpu.SMEM)] + [whole] * (5 * len(sizes)),
        out_specs=[whole] * 3,
        compiler_params=pltpu.CompilerParams(vmem_limit_bytes=VMEM_LIMIT),
        name="finish",
    )(order, *(part for kind in parts for part in kind))


def body(query_tokens, key_tokens, value_tokens, forward_out, out_grad, log_norm, window_ids):
    rows, features = query_tokens.shape
    heads = log_norm.shape[0]
    tiles = lax.axis_size("tile")
    beside = [(i, (i + tiles // 2) % tiles) for i in range(tiles)]
    up = [(i, i + 1) for i in range(tiles - 1) if (i + 1) % GRID_WIDTH]
    down = [(b, a) for a, b in up]
    move = lambda value, pairs: lax.ppermute(value, "tile", pairs)
    sizes = (2,) * (heads // 2)
    order = jnp.arange(heads, dtype=jnp.int32)
    *own, own_aux, send_aux = pack(order, window_ids[:, 0, :], query_tokens, out_grad, forward_out, log_norm, sizes)
    other_aux = move(send_aux, beside)
    other = [move(chunk, beside) for chunk in own]
    keys = (key_tokens, move(key_tokens, up), move(key_tokens, down))
    values = (value_tokens, move(value_tokens, up), move(value_tokens, down))
    parts = [[] for _ in range(5)]
    base = 0
    for c, count in enumerate(sizes):
        own_query, other_query, own_pair, left_pair, right_pair = terms(
            order, own[c], own_aux, other[c], other_aux, keys, values, base
        )
        made = (own_query, move(other_query, beside), own_pair, move(right_pair, up), move(left_pair, down))
        for part, value in zip(parts, made):
            part.append(value)
        base += count
    return tuple(finish(order, parts, sizes, rows, features))


def solution(mesh):
    placed = (
        P(("group", "tile"), None),
        P(("group", "tile"), None),
        P(("group", "tile"), None),
        P(("group", "tile"), None),
        P(("group", "tile"), None),
        P(None, ("group", "tile")),
        P(None, "tile", None),
    )
    return jax.shard_map(
        body,
        mesh=mesh,
        in_specs=placed,
        out_specs=(
            P(("group", "tile"), None),
            P(("group", "tile"), None),
            P(("group", "tile"), None),
        ),
        check_vma=False,
    )
```

```python
import functools
import math

import jax
import jax.numpy as jnp
from jax import lax
from jax.experimental import pallas as pl
from jax.experimental.pallas import tpu as pltpu
from jax.sharding import PartitionSpec as P

GRID_WIDTH = 8
ABSENT = 1e30
LOG2E = 1.4426950408889634
NT = (((1,), (1,)), ((), ()))
TN = (((0,), (0,)), ((), ()))
VMEM_LIMIT = 24 * 2**20
EXTRA = 16
SPARED = 5


def dot(a, b, dims=(((1,), (0,)), ((), ()))):
    return lax.dot_general(a, b, dims, preferred_element_type=jnp.float32)


def short(value):
    return value.astype(jnp.bfloat16).astype(jnp.float32)


WHOLE = pl.BlockSpec(memory_space=pltpu.VMEM)
SCALAR = pl.BlockSpec(memory_space=pltpu.SMEM)
ANY = pl.BlockSpec(memory_space=pl.ANY)


def kernel_call(kernel, name, in_specs, out_specs, out_shape, **more):
    return pl.pallas_call(
        kernel,
        out_shape=out_shape,
        in_specs=in_specs,
        out_specs=out_specs,
        compiler_params=pltpu.CompilerParams(vmem_limit_bytes=VMEM_LIMIT),
        name=name,
        **more,
    )


def columns(order, place, size):
    return pl.ds(pl.multiple_of(order[place] * size, size), size)


def write_order(window, order):
    heads = window.shape[0]
    on = [(window[h, 0] >= 0).astype(jnp.int32) for h in range(heads)]
    first, last = jnp.int32(0), sum(on)
    for h in range(heads):
        order[jnp.where(on[h] > 0, first, last)] = jnp.int32(h)
        first, last = first + on[h], last + 1 - on[h]


def pack_kernel(window, log_norm, query, grad, out, key, value, *refs, sizes):
    chunks, (order, own_aux, pair, rows32) = refs[: len(sizes)], refs[len(sizes) :]
    heads, rows = log_norm.shape
    size = query.shape[1] // heads
    write_order(window, order)
    pair[0] = key[...]
    pair[1] = value[...]
    rows32[...] = jnp.zeros(rows32.shape, jnp.float32)
    ones = jnp.ones((8, size), jnp.bfloat16)
    lane = lax.broadcasted_iota(jnp.int32, (1, size), 1)

    def flag_row(head, slots, lane):
        row = jnp.zeros(lane.shape, jnp.float32)
        for place, slot in slots:
            row = jnp.where(lane == place, jnp.where(window[head, slot] < 0, ABSENT, 0.0), row)
        return row

    def describe(place, _):
        head = order[place]
        here = columns(order, place, size)
        product = grad[:, here].astype(jnp.float32) * out[:, here].astype(jnp.float32)
        high = short(product)
        low = product - high
        delta = dot(ones, high.astype(jnp.bfloat16), NT) + dot(ones, low.astype(jnp.bfloat16), NT)
        own_aux[place, 0:1, :rows] = log_norm[pl.ds(head, 1), :] * LOG2E
        own_aux[place, 1:2, :rows] = delta[0:1]
        own_aux[place, 2:3, :size] = flag_row(head, ((1, 1), (2, 2)), lane)
        return 0

    lax.fori_loop(0, heads, describe, 0)
    base = 0
    for chunk, count in zip(chunks, sizes):

        def fill(i, _, chunk=chunk, base=base):
            place = base + i
            here = columns(order, place, size)
            chunk[i, :rows] = query[:, here]
            chunk[i, rows : 2 * rows] = grad[:, here]
            both = own_aux[place, 0:2, :rows]
            one = short(both)
            two = short(both - one)
            for k, part in enumerate((one, two, both - one - two)):
                rows32[4 * k : 4 * k + 2, :] = part[:, :size]
                rows32[4 * k + 2 : 4 * k + 4, : rows - size] = part[:, size:]
            rows32[12:13, :] = flag_row(order[place], ((0, 0), (1, 3), (2, 4)), lane)
            chunk[i, 2 * rows :] = rows32[...].astype(jnp.bfloat16)
            return 0

        lax.fori_loop(0, count, fill, 0)
        base += count


def pack(window, log_norm, query, grad, out, key, value, sizes):
    heads, rows = log_norm.shape
    features = query.shape[1]
    size = features // heads
    lanes = -(-rows // 128) * 128
    bf16 = jnp.bfloat16
    return kernel_call(
        functools.partial(pack_kernel, sizes=sizes),
        "pack",
        [SCALAR] + [WHOLE] * 6,
        [WHOLE] * len(sizes) + [SCALAR, WHOLE, WHOLE],
        [jax.ShapeDtypeStruct((n, 2 * rows + EXTRA, size), bf16) for n in sizes]
        + [
            jax.ShapeDtypeStruct((heads,), jnp.int32),
            jax.ShapeDtypeStruct((heads, 4, lanes), jnp.float32),
            jax.ShapeDtypeStruct((2, rows, features), bf16),
        ],
        scratch_shapes=[pltpu.VMEM((EXTRA, size), jnp.float32)],
    )(window, log_norm, query, grad, out, key, value)


def terms_kernel(order, own_aux, query, grad, *refs, base, both, score_scale):
    rows = query.shape[0]
    refs = list(refs)
    other = refs.pop(0) if both else None
    key, value, lower, upper = refs[:4]
    refs = refs[4:]
    own_query = refs.pop(0)
    other_query = refs.pop(0) if both else None
    count, _, _, size = refs[0].shape

    def one_head(i, _):
        place = base + i
        here = columns(order, place, size)
        mine = own_aux[place]
        queries, grads, delta = query[:, here], grad[:, here], mine[1:2, :rows]
        norms = [mine[0:1, :rows] + (mine[2:3, j : j + 1] if j else 0.0) for j in range(3)]
        if both:
            extra = other[i, 2 * rows :].astype(jnp.float32)
            theirs = jnp.concatenate(
                [
                    extra[0:2] + extra[4:6] + extra[8:10],
                    (extra[2:4] + extra[6:8] + extra[10:12])[:, : rows - size],
                ],
                axis=1,
            )
            norms = [
                jnp.concatenate([norms[j], theirs[0:1] + extra[12:13, j : j + 1]], axis=1) for j in range(3)
            ]
            queries = jnp.concatenate([queries, other[i, :rows]], axis=0)
            grads = jnp.concatenate([grads, other[i, rows : 2 * rows]], axis=0)
            delta = jnp.concatenate([delta, theirs[1:2]], axis=1)
        keys = jnp.concatenate([key[:, here], lower[0, :, here], upper[0, :, here]], axis=0)
        values = jnp.concatenate([value[:, here], lower[1, :, here], upper[1, :, here]], axis=0)
        norm = jnp.concatenate([jnp.broadcast_to(row, (rows, row.shape[1])) for row in norms], axis=0)
        weights = jnp.exp2(dot(keys, queries, NT) * (score_scale * LOG2E) - norm)
        value_terms = dot(weights.astype(jnp.bfloat16), grads).astype(jnp.bfloat16)
        grad_scores = (weights * (dot(values, grads, NT) - delta)).astype(jnp.bfloat16)
        key_terms = (dot(grad_scores, queries) * score_scale).astype(jnp.bfloat16)
        query_terms = (dot(grad_scores, keys, TN) * score_scale).astype(jnp.bfloat16)
        own_query[i] = query_terms[:rows]
        if both:
            other_query[i] = query_terms[rows:]
        for j in range(3):
            refs[j][i, 0] = key_terms[j * rows : (j + 1) * rows]
            refs[j][i, 1] = value_terms[j * rows : (j + 1) * rows]
        return 0

    lax.fori_loop(0, count, one_head, 0)


def terms(order, own_aux, query, grad, other, key, value, lower, upper, base, count):
    rows, features = query.shape
    size = features // own_aux.shape[0]
    both = other is not None
    pair = jax.ShapeDtypeStruct((count, 2, rows, size), jnp.bfloat16)
    single = jax.ShapeDtypeStruct((count, rows, size), jnp.bfloat16)
    pairs = count * 3 * (1 + both)
    return kernel_call(
        functools.partial(terms_kernel, base=base, both=both, score_scale=1.0 / math.sqrt(size)),
        "terms",
        [SCALAR] + [WHOLE] * (7 + both),
        [WHOLE] * (4 + both),
        [single] * (1 + both) + [pair] * 3,
        cost_estimate=pl.CostEstimate(
            flops=pairs * 10 * rows * rows * size,
            bytes_accessed=count * 18 * rows * size * 2,
            transcendentals=pairs * rows * rows,
        ),
    )(order, own_aux, query, grad, *[other] * both, key, value, lower, upper)


def finish_kernel(order, *refs, sizes, sent):
    n = len(sizes)
    refs = list(refs)
    take = lambda count: [refs.pop(0) for _ in range(count)]
    own_query, back_query, own, left, right = take(n), take(sent), take(n), take(n), take(n)
    query_out, key_out, value_out = refs
    size = own_query[0].shape[2]
    base = 0
    for c, count in enumerate(sizes):

        def one_head(i, _, c=c, base=base):
            here = columns(order, base + i, size)
            query = own_query[c][i]
            if c < sent:
                query = (query.astype(jnp.float32) + back_query[c][i].astype(jnp.float32)).astype(jnp.bfloat16)
            query_out[:, here] = query
            for k, result in ((0, key_out), (1, value_out)):
                total = (
                    own[c][i, k].astype(jnp.float32)
                    + left[c][i, k].astype(jnp.float32)
                    + right[c][i, k].astype(jnp.float32)
                )
                result[:, here] = total.astype(jnp.bfloat16)
            return 0

        lax.fori_loop(0, count, one_head, 0)
        base += count


def finish(order, parts, sizes, rows, features):
    return kernel_call(
        functools.partial(finish_kernel, sizes=sizes, sent=len(parts[1])),
        "finish",
        [SCALAR] + [WHOLE] * sum(map(len, parts)),
        [WHOLE] * 3,
        [jax.ShapeDtypeStruct((rows, features), jnp.bfloat16)] * 3,
    )(order, *(part for kind in parts for part in kind))


def split(count):
    if count <= 2:
        return (count,) * (count > 0)
    if count <= 5:
        return (count - count // 2, count // 2)
    return (count - 2 * (count // 3), count // 3, count // 3)


def exchange(count, window, log_norm, query, grad, out, key, value):
    rows, features = query.shape
    heads = log_norm.shape[0]
    tiles = lax.axis_size("tile")
    beside = [(i, (i + tiles // 2) % tiles) for i in range(tiles)]
    up = [(i, i + 1) for i in range(tiles - 1) if (i + 1) % GRID_WIDTH]
    down = [(b, a) for a, b in up]
    move = lambda value, pairs: lax.ppermute(value, "tile", pairs)
    sizes = split(count)
    *sends, order, own_aux, pair = pack(window, log_norm, query, grad, out, key, value, sizes)
    others = [move(send, beside) for send in sends]
    lower, upper = move(pair, up), move(pair, down)
    parts = [[] for _ in range(5)]
    if count < heads:
        sizes, others = sizes + (heads - count,), others + [None]
    base = 0
    for size, other in zip(sizes, others):
        made = list(terms(order, own_aux, query, grad, other, key, value, lower, upper, base, size))
        parts[0].append(made.pop(0))
        if other is not None:
            parts[1].append(move(made.pop(0), beside))
        parts[2].append(made[0])
        parts[3].append(move(made[2], up))
        parts[4].append(move(made[1], down))
        base += size
    return tuple(finish(order, parts, sizes, rows, features))


def body(query_tokens, key_tokens, value_tokens, forward_out, out_grad, log_norm, window_ids):
    window = window_ids[:, 0, :]
    heads = log_norm.shape[0]
    least = max(heads - SPARED, 1)
    count = jnp.sum((window[:, 0] >= 0).astype(jnp.int32))
    return lax.switch(
        jnp.maximum(count - least, 0),
        [functools.partial(exchange, n) for n in range(least, heads + 1)],
        window,
        log_norm,
        query_tokens,
        out_grad,
        forward_out,
        key_tokens,
        value_tokens,
    )


def solution(mesh):
    placed = (
        P(("group", "tile"), None),
        P(("group", "tile"), None),
        P(("group", "tile"), None),
        P(("group", "tile"), None),
        P(("group", "tile"), None),
        P(None, ("group", "tile")),
        P(None, "tile", None),
    )
    return jax.shard_map(
        body,
        mesh=mesh,
        in_specs=placed,
        out_specs=(
            P(("group", "tile"), None),
            P(("group", "tile"), None),
            P(("group", "tile"), None),
        ),
        check_vma=False,
    )
```

```python
import functools
import math

import jax
import jax.numpy as jnp
from jax import lax
from jax.experimental import pallas as pl
from jax.experimental.pallas import tpu as pltpu
from jax.sharding import PartitionSpec as P

GRID_WIDTH = 8
ABSENT = 1e30
LOG2E = 1.4426950408889634
NT = (((1,), (1,)), ((), ()))
TN = (((0,), (0,)), ((), ()))
VMEM_LIMIT = 24 * 2**20
EXTRA = 16
SPARED = 5
LONG = 3 * 10**10


def dot(a, b, dims=(((1,), (0,)), ((), ()))):
    return lax.dot_general(a, b, dims, preferred_element_type=jnp.float32)


def short(value):
    return value.astype(jnp.bfloat16).astype(jnp.float32)


WHOLE = pl.BlockSpec(memory_space=pltpu.VMEM)
SCALAR = pl.BlockSpec(memory_space=pltpu.SMEM)
ANY = pl.BlockSpec(memory_space=pl.ANY)


def kernel_call(kernel, name, in_specs, out_specs, out_shape, cost=1, **more):
    return pl.pallas_call(
        kernel,
        out_shape=out_shape,
        in_specs=in_specs,
        out_specs=out_specs,
        compiler_params=pltpu.CompilerParams(vmem_limit_bytes=VMEM_LIMIT),
        cost_estimate=pl.CostEstimate(flops=cost, bytes_accessed=1, transcendentals=0),
        name=name,
        **more,
    )


def columns(order, place, size):
    return pl.ds(pl.multiple_of(order[place] * size, size), size)


def write_order(window, order):
    heads = window.shape[0]
    on = [(window[h, 0] >= 0).astype(jnp.int32) for h in range(heads)]
    first, last = jnp.int32(0), sum(on)
    for h in range(heads):
        order[jnp.where(on[h] > 0, first, last)] = jnp.int32(h)
        first, last = first + on[h], last + 1 - on[h]


def flag_row(window, head, slots, lane):
    row = jnp.zeros(lane.shape, jnp.float32)
    for place, slot in slots:
        row = jnp.where(lane == place, jnp.where(window[head, slot] < 0, ABSENT, 0.0), row)
    return row


def describe(log_norm, grad, out, head, here, ones):
    product = grad[:, here].astype(jnp.float32) * out[:, here].astype(jnp.float32)
    high = short(product)
    both = jnp.concatenate([high.astype(jnp.bfloat16), (product - high).astype(jnp.bfloat16)], axis=1)
    return log_norm[pl.ds(head, 1), :] * LOG2E, dot(ones, both, NT)[0:1]


def fill(chunk, i, window, query, grad, head, here, lines, rows32, lane):
    rows, size = query.shape[0], chunk.shape[2]
    chunk[i, :rows] = query[:, here]
    chunk[i, rows : 2 * rows] = grad[:, here]
    one = short(lines)
    two = short(lines - one)
    for k, part in enumerate((one, two, lines - one - two)):
        rows32[4 * k : 4 * k + 2, :] = part[:, :size]
        rows32[4 * k + 2 : 4 * k + 4, : rows - size] = part[:, size:]
    rows32[12:13, :] = flag_row(window, head, ((0, 0), (1, 3), (2, 4)), lane)
    chunk[i, 2 * rows :] = rows32[...].astype(jnp.bfloat16)


def first_pack_kernel(window, log_norm, query, grad, out, key, value, chunk, pair, order, rows32):
    heads = log_norm.shape[0]
    size = query.shape[1] // heads
    write_order(window, order)
    rows32[...] = jnp.zeros(rows32.shape, jnp.float32)
    ones = jnp.ones((8, 2 * size), jnp.bfloat16)
    lane = lax.broadcasted_iota(jnp.int32, (1, size), 1)

    def one_head(i, _):
        head, here = order[i], columns(order, i, size)
        lines = jnp.concatenate(describe(log_norm, grad, out, head, here, ones), axis=0)
        fill(chunk, i, window, query, grad, head, here, lines, rows32, lane)
        pair[i, 0], pair[i, 1] = key[:, here], value[:, here]
        return 0

    lax.fori_loop(0, chunk.shape[0], one_head, 0)


def first_pack(window, log_norm, query, grad, out, key, value, count):
    heads, rows = log_norm.shape
    size = query.shape[1] // heads
    return kernel_call(
        first_pack_kernel,
        "first_pack",
        [SCALAR] + [WHOLE] * 6,
        [WHOLE, WHOLE, SCALAR],
        [
            jax.ShapeDtypeStruct((count, 2 * rows + EXTRA, size), jnp.bfloat16),
            jax.ShapeDtypeStruct((count, 2, rows, size), jnp.bfloat16),
            jax.ShapeDtypeStruct((heads,), jnp.int32),
        ],
        scratch_shapes=[pltpu.VMEM((EXTRA, size), jnp.float32)],
    )(window, log_norm, query, grad, out, key, value)


def pack_kernel(order, window, log_norm, query, grad, out, key, value, *refs, sizes, base):
    chunks, (own_aux, pair, rows32) = refs[: len(sizes)], refs[len(sizes) :]
    heads, rows = log_norm.shape
    skipped = base
    size = query.shape[1] // heads
    rows32[...] = jnp.zeros(rows32.shape, jnp.float32)
    ones = jnp.ones((8, 2 * size), jnp.bfloat16)
    lane = lax.broadcasted_iota(jnp.int32, (1, size), 1)

    def one_head(place, _):
        head, here = order[place], columns(order, place, size)
        norm, delta = describe(log_norm, grad, out, head, here, ones)
        own_aux[place, 0:1, :rows] = norm
        own_aux[place, 1:2, :rows] = delta
        own_aux[place, 2:3, :size] = flag_row(window, head, ((1, 1), (2, 2)), lane)

        @pl.when(place >= skipped)
        def _():
            pair[place - skipped, 0], pair[place - skipped, 1] = key[:, here], value[:, here]

        return 0

    lax.fori_loop(0, heads, one_head, 0)
    for chunk, count in zip(chunks, sizes):

        def one_send(i, _, chunk=chunk, base=base):
            head, here = order[base + i], columns(order, base + i, size)
            lines = own_aux[base + i, 0:2, :rows]
            fill(chunk, i, window, query, grad, head, here, lines, rows32, lane)
            return 0

        lax.fori_loop(0, count, one_send, 0)
        base += count


def pack(order, window, log_norm, query, grad, out, key, value, sizes, base):
    heads, rows = log_norm.shape
    features = query.shape[1]
    size = features // heads
    lanes = -(-rows // 128) * 128
    bf16 = jnp.bfloat16
    return kernel_call(
        functools.partial(pack_kernel, sizes=sizes, base=base),
        "pack",
        [SCALAR] * 2 + [WHOLE] * 6,
        [WHOLE] * (len(sizes) + 2),
        [jax.ShapeDtypeStruct((n, 2 * rows + EXTRA, size), bf16) for n in sizes]
        + [
            jax.ShapeDtypeStruct((heads, 4, lanes), jnp.float32),
            jax.ShapeDtypeStruct((heads - base, 2, rows, size), bf16),
        ],
        scratch_shapes=[pltpu.VMEM((EXTRA, size), jnp.float32)],
    )(order, window, log_norm, query, grad, out, key, value)


def terms_kernel(order, own_aux, query, grad, *refs, base, start, near, both, kept, score_scale):
    rows = query.shape[0]
    refs = list(refs)
    other = refs.pop(0) if both else None
    key, value, lower, upper = refs[:4]
    earlier, refs = refs[4 : 4 + 2 * kept], refs[4 + 2 * kept :]
    own_query = refs.pop(0)
    other_query = refs.pop(0) if both else None
    count, _, _, size = refs[0].shape
    shift = 0
    for j in range(kept):
        for side in range(2):
            refs[1 + side][shift : shift + earlier[2 * j].shape[0]] = earlier[2 * j + side][...]
        shift += earlier[2 * j].shape[0]

    def one_head(i, _):
        place = base + i
        here = columns(order, place, size)
        mine = own_aux[place]
        queries, grads, delta = query[:, here], grad[:, here], mine[1:2, :rows]
        norms = [mine[0:1, :rows] + (mine[2:3, j : j + 1] if j else 0.0) for j in range(3)]
        if both:
            extra = other[start + i, 2 * rows :].astype(jnp.float32)
            theirs = jnp.concatenate(
                [
                    extra[0:2] + extra[4:6] + extra[8:10],
                    (extra[2:4] + extra[6:8] + extra[10:12])[:, : rows - size],
                ],
                axis=1,
            )
            norms = [
                jnp.concatenate([norms[j], theirs[0:1] + extra[12:13, j : j + 1]], axis=1) for j in range(3)
            ]
            queries = jnp.concatenate([queries, other[start + i, :rows]], axis=0)
            grads = jnp.concatenate([grads, other[start + i, rows : 2 * rows]], axis=0)
            delta = jnp.concatenate([delta, theirs[1:2]], axis=1)
        keys = jnp.concatenate([key[:, here], lower[near + i, 0], upper[near + i, 0]], axis=0)
        values = jnp.concatenate([value[:, here], lower[near + i, 1], upper[near + i, 1]], axis=0)
        norm = jnp.concatenate([jnp.broadcast_to(row, (rows, row.shape[1])) for row in norms], axis=0)
        weights = jnp.exp2(dot(keys, queries, NT) * (score_scale * LOG2E) - norm)
        value_terms = dot(weights.astype(jnp.bfloat16), grads).astype(jnp.bfloat16)
        grad_scores = (weights * (dot(values, grads, NT) - delta)).astype(jnp.bfloat16)
        key_terms = (dot(grad_scores, queries) * score_scale).astype(jnp.bfloat16)
        query_terms = (dot(grad_scores, keys, TN) * score_scale).astype(jnp.bfloat16)
        own_query[i] = query_terms[:rows]
        if both:
            other_query[i] = query_terms[rows:]
        for j in range(3):
            to = i + shift if j else i
            refs[j][to, 0] = key_terms[j * rows : (j + 1) * rows]
            refs[j][to, 1] = value_terms[j * rows : (j + 1) * rows]
        return 0

    lax.fori_loop(0, count, one_head, 0)


def terms(order, own_aux, query, grad, other, key, value, lower, upper, base, count, start=0, near=0, earlier=(), cost=1):
    rows, features = query.shape
    size = features // own_aux.shape[0]
    both = other is not None
    pair = jax.ShapeDtypeStruct((count, 2, rows, size), jnp.bfloat16)
    total = count + sum(low.shape[0] for low, _ in earlier)
    side = jax.ShapeDtypeStruct((total, 2, rows, size), jnp.bfloat16)
    single = jax.ShapeDtypeStruct((count, rows, size), jnp.bfloat16)
    return kernel_call(
        functools.partial(terms_kernel, base=base, start=start, near=near, both=both, kept=len(earlier), score_scale=1.0 / math.sqrt(size)),
        "terms",
        [SCALAR] + [WHOLE] * (7 + both + 2 * len(earlier)),
        [WHOLE] * (4 + both),
        [single] * (1 + both) + [pair, side, side],
        cost=cost,
    )(order, own_aux, query, grad, *[other] * both, key, value, lower, upper, *(x for two in earlier for x in two))


def finish_query_kernel(order, *refs, plan):
    result = refs[-1]
    size = refs[0].shape[2]
    for base, count, own, back in plan:

        def one_head(i, _, base=base, own=own, back=back):
            total = refs[own][i]
            if back is not None:
                total = (total.astype(jnp.float32) + refs[back][i].astype(jnp.float32)).astype(jnp.bfloat16)
            result[:, columns(order, base + i, size)] = total
            return 0

        lax.fori_loop(0, count, one_head, 0)


def finish_pair_kernel(order, *refs, plan):
    size = refs[0].shape[3]
    for base, count, own, lower, upper, shift in plan:

        def one_head(i, _, base=base, own=own, lower=lower, upper=upper, shift=shift):
            here = columns(order, base + i, size)
            for k, result in enumerate(refs[-2:]):
                total = (
                    refs[own][i, k].astype(jnp.float32)
                    + refs[lower][i + shift, k].astype(jnp.float32)
                    + refs[upper][i + shift, k].astype(jnp.float32)
                )
                result[:, here] = total.astype(jnp.bfloat16)
            return 0

        lax.fori_loop(0, count, one_head, 0)


def finish(kernel, order, operands, plan, rows, features, count, **more):
    return kernel_call(
        functools.partial(kernel, plan=tuple(plan)),
        "finish",
        [SCALAR] + [WHOLE] * len(operands),
        [WHOLE] * count,
        [jax.ShapeDtypeStruct((rows, features), jnp.bfloat16)] * count,
        **more,
    )(order, *operands)


def once_here_kernel(order, *refs):
    result = refs[-1]
    for i in range(order.shape[0]):
        result[i] = order[i]


def once_here(order, *values):
    return kernel_call(
        once_here_kernel,
        "once_here",
        [SCALAR] + [ANY] * len(values),
        SCALAR,
        jax.ShapeDtypeStruct(order.shape, order.dtype),
        cost=LONG,
    )(order, *values)


def after(value, other):
    return lax.optimization_barrier((value, other))[0]


def split(count):
    first = count - count // 2 - (count > 6)
    return (first, count - first) if count > first else (first,)


def exchange(count, window, log_norm, query, grad, out, key, value):
    rows, features = query.shape
    heads = log_norm.shape[0]
    tiles = lax.axis_size("tile")
    beside = [(i, (i + tiles // 2) % tiles) for i in range(tiles)]
    up = [(i, i + 1) for i in range(tiles - 1) if (i + 1) % GRID_WIDTH]
    down = [(b, a) for a, b in up]
    move = lambda value, pairs: lax.ppermute(value, "tile", pairs)
    sizes = split(count)
    first, first_pair, order = first_pack(window, log_norm, query, grad, out, key, value, sizes[0])
    *later, own_aux, pair = pack(order, window, log_norm, query, grad, out, key, value, sizes[1:], sizes[0])
    first_sides = move(first_pair, up), move(first_pair, down)
    sides = move(pair, up), move(pair, down)
    others = [move(first, beside)]
    for send in later:
        others.append(move(after(send, others[0]), beside))
    jobs = [(sum(sizes[:c]), size, other, c > 0 or count == heads) for c, (size, other) in enumerate(zip(sizes, others))]
    if count < heads:
        jobs.insert(1, (count, heads - count, None, True))
    query_parts, query_plan, pair_parts, pair_plan, waiting, held = [], [], [], [], [], []

    def add(operands, operand):
        operands.append(operand)
        return len(operands) - 1

    below = above = None
    later_order = order
    own_query = order
    for base, size, other, send in jobs:
        own_query, *made = terms(
            once_here(order, other) if base == 0 else after(order, own_query),
            own_aux,
            query,
            grad,
            other,
            key,
            value,
            *(sides if base else first_sides),
            base,
            size,
            near=max(base - sizes[0], 0),
            earlier=waiting if send else (),
            cost=LONG if other is not None and base else 1,
        )
        back = None if other is None else add(query_parts, move(made.pop(0), beside))
        query_plan.append((base, size, add(query_parts, own_query), back))
        held.append((base, size, add(pair_parts, made[0])))
        waiting.append((made[1], made[2]))
        if send:
            sent = (made[2], made[1])
            if below is not None:
                later_order = once_here(order, query_parts[0], below, above)
                sent = after(sent, later_order)
            below, above = move(sent[0], up), move(sent[1], down)
            places = add(pair_parts, below), add(pair_parts, above)
            shift = 0
            for entry in held:
                pair_plan.append((*entry, *places, shift))
                shift += entry[1]
            waiting, held = [], []
    (grad_query,) = finish(
        finish_query_kernel, later_order, query_parts, query_plan, rows, features, 1, cost=LONG
    )
    pair_parts = after(pair_parts, grad_query)
    return grad_query, *finish(finish_pair_kernel, order, pair_parts, pair_plan, rows, features, 2)


def body(query_tokens, key_tokens, value_tokens, forward_out, out_grad, log_norm, window_ids):
    window = window_ids[:, 0, :]
    heads = log_norm.shape[0]
    least = max(heads - SPARED, 1)
    count = jnp.sum((window[:, 0] >= 0).astype(jnp.int32))
    return lax.switch(
        jnp.maximum(count - least, 0),
        [functools.partial(exchange, n) for n in range(least, heads + 1)],
        window,
        log_norm,
        query_tokens,
        out_grad,
        forward_out,
        key_tokens,
        value_tokens,
    )


def solution(mesh):
    placed = (
        P(("group", "tile"), None),
        P(("group", "tile"), None),
        P(("group", "tile"), None),
        P(("group", "tile"), None),
        P(("group", "tile"), None),
        P(None, ("group", "tile")),
        P(None, "tile", None),
    )
    return jax.shard_map(
        body,
        mesh=mesh,
        in_specs=placed,
        out_specs=(
            P(("group", "tile"), None),
            P(("group", "tile"), None),
            P(("group", "tile"), None),
        ),
        check_vma=False,
    )
```

```python
import functools
import math

import jax
import jax.numpy as jnp
from jax import lax
from jax.experimental import pallas as pl
from jax.experimental.pallas import tpu as pltpu
from jax.sharding import PartitionSpec as P

GRID_WIDTH = 8
ABSENT = 1e30
LOG2E = 1.4426950408889634
NT = (((1,), (1,)), ((), ()))
TN = (((0,), (0,)), ((), ()))
VMEM_LIMIT = 24 * 2**20
EXTRA = 16
SPARED = 4
LONG = 3 * 10**10


def dot(a, b, dims=(((1,), (0,)), ((), ()))):
    return lax.dot_general(a, b, dims, preferred_element_type=jnp.float32)


def short(value):
    return value.astype(jnp.bfloat16).astype(jnp.float32)


WHOLE = pl.BlockSpec(memory_space=pltpu.VMEM)
SCALAR = pl.BlockSpec(memory_space=pltpu.SMEM)
ANY = pl.BlockSpec(memory_space=pl.ANY)


def kernel_call(kernel, name, in_specs, out_specs, out_shape, cost=1, effects=False, **more):
    return pl.pallas_call(
        kernel,
        out_shape=out_shape,
        in_specs=in_specs,
        out_specs=out_specs,
        compiler_params=pltpu.CompilerParams(vmem_limit_bytes=VMEM_LIMIT, has_side_effects=effects),
        cost_estimate=pl.CostEstimate(flops=cost, bytes_accessed=1, transcendentals=0),
        name=name,
        **more,
    )


def columns(order, place, size):
    return pl.ds(pl.multiple_of(order[place] * size, size), size)


def write_order(window, order):
    heads = window.shape[0]
    on = [(window[h, 0] >= 0).astype(jnp.int32) for h in range(heads)]
    first, last = jnp.int32(0), sum(on)
    for h in range(heads):
        order[jnp.where(on[h] > 0, first, last)] = jnp.int32(h)
        first, last = first + on[h], last + 1 - on[h]


def flag_row(window, head, slots, lane):
    row = jnp.zeros(lane.shape, jnp.float32)
    for place, slot in slots:
        row = jnp.where(lane == place, jnp.where(window[head, slot] < 0, ABSENT, 0.0), row)
    return row


def describe(log_norm, grad, out, head, here, ones):
    product = grad[:, here].astype(jnp.float32) * out[:, here].astype(jnp.float32)
    high = short(product)
    both = jnp.concatenate([high.astype(jnp.bfloat16), (product - high).astype(jnp.bfloat16)], axis=1)
    return log_norm[pl.ds(head, 1), :] * LOG2E, dot(ones, both, NT)[0:1]


def fill(chunk, i, window, query, grad, head, here, lines, rows32, lane):
    rows, size = query.shape[0], chunk.shape[2]
    chunk[i, :rows] = query[:, here]
    chunk[i, rows : 2 * rows] = grad[:, here]
    one = short(lines)
    two = short(lines - one)
    for k, part in enumerate((one, two, lines - one - two)):
        rows32[4 * k : 4 * k + 2, :] = part[:, :size]
        rows32[4 * k + 2 : 4 * k + 4, : rows - size] = part[:, size:]
    rows32[12:13, :] = flag_row(window, head, ((0, 0), (1, 3), (2, 4)), lane)
    chunk[i, 2 * rows :] = rows32[...].astype(jnp.bfloat16)


def fill_pair(pair, order, key, value, base, count, to):
    size = pair.shape[3]

    def one_head(i, _):
        here = columns(order, base + i, size)
        pair[to + i, 0], pair[to + i, 1] = key[:, here], value[:, here]
        return 0

    lax.fori_loop(0, count, one_head, 0)


def first_pack_kernel(window, log_norm, query, grad, out, key, value, chunk, pair, order, rows32, *, sent):
    heads = log_norm.shape[0]
    size = query.shape[1] // heads
    write_order(window, order)
    rows32[...] = jnp.zeros(rows32.shape, jnp.float32)
    ones = jnp.ones((8, 2 * size), jnp.bfloat16)
    lane = lax.broadcasted_iota(jnp.int32, (1, size), 1)

    def one_head(i, _):
        head, here = order[i], columns(order, i, size)
        lines = jnp.concatenate(describe(log_norm, grad, out, head, here, ones), axis=0)
        fill(chunk, i, window, query, grad, head, here, lines, rows32, lane)
        return 0

    lax.fori_loop(0, chunk.shape[0], one_head, 0)
    fill_pair(pair, order, key, value, 0, chunk.shape[0], 0)
    fill_pair(pair, order, key, value, sent, heads - sent, chunk.shape[0])


def first_pack(window, log_norm, query, grad, out, key, value, count, sent):
    heads, rows = log_norm.shape
    size = query.shape[1] // heads
    return kernel_call(
        functools.partial(first_pack_kernel, sent=sent),
        "first_pack",
        [SCALAR] + [WHOLE] * 6,
        [WHOLE, WHOLE, SCALAR],
        [
            jax.ShapeDtypeStruct((count, 2 * rows + EXTRA, size), jnp.bfloat16),
            jax.ShapeDtypeStruct((count + heads - sent, 2, rows, size), jnp.bfloat16),
            jax.ShapeDtypeStruct((heads,), jnp.int32),
        ],
        scratch_shapes=[pltpu.VMEM((EXTRA, size), jnp.float32)],
    )(window, log_norm, query, grad, out, key, value)


def pack_kernel(order, window, log_norm, query, grad, out, key, value, *refs, sizes, base):
    chunks, (own_aux, pair, rows32) = refs[: len(sizes)], refs[len(sizes) :]
    heads, rows = log_norm.shape
    size = query.shape[1] // heads
    rows32[...] = jnp.zeros(rows32.shape, jnp.float32)
    ones = jnp.ones((8, 2 * size), jnp.bfloat16)
    lane = lax.broadcasted_iota(jnp.int32, (1, size), 1)

    def one_head(place, _):
        head, here = order[place], columns(order, place, size)
        norm, delta = describe(log_norm, grad, out, head, here, ones)
        own_aux[place, 0:1, :rows] = norm
        own_aux[place, 1:2, :rows] = delta
        own_aux[place, 2:3, :size] = flag_row(window, head, ((1, 1), (2, 2)), lane)
        return 0

    lax.fori_loop(0, heads, one_head, 0)
    fill_pair(pair, order, key, value, base, sum(sizes), 0)
    for chunk, count in zip(chunks, sizes):

        def one_send(i, _, chunk=chunk, base=base):
            head, here = order[base + i], columns(order, base + i, size)
            lines = own_aux[base + i, 0:2, :rows]
            fill(chunk, i, window, query, grad, head, here, lines, rows32, lane)
            return 0

        lax.fori_loop(0, count, one_send, 0)
        base += count


def pack(order, window, log_norm, query, grad, out, key, value, sizes, base):
    heads, rows = log_norm.shape
    features = query.shape[1]
    size = features // heads
    lanes = -(-rows // 128) * 128
    bf16 = jnp.bfloat16
    return kernel_call(
        functools.partial(pack_kernel, sizes=sizes, base=base),
        "pack",
        [SCALAR] * 2 + [WHOLE] * 6,
        [WHOLE] * (len(sizes) + 2),
        [jax.ShapeDtypeStruct((n, 2 * rows + EXTRA, size), bf16) for n in sizes]
        + [
            jax.ShapeDtypeStruct((heads, 4, lanes), jnp.float32),
            jax.ShapeDtypeStruct((sum(sizes), 2, rows, size), bf16),
        ],
        scratch_shapes=[pltpu.VMEM((EXTRA, size), jnp.float32)],
    )(order, window, log_norm, query, grad, out, key, value)


def terms_kernel(order, own_aux, query, grad, *refs, base, start, near, both, kept, score_scale):
    rows = query.shape[0]
    refs = list(refs)
    other = refs.pop(0) if both else None
    key, value, lower, upper = refs[:4]
    earlier, refs = refs[4 : 4 + 2 * kept], refs[4 + 2 * kept :]
    own_query = refs.pop(0)
    other_query = refs.pop(0) if both else None
    count, _, _, size = refs[0].shape
    shift = 0
    for j in range(kept):
        for side in range(2):
            refs[1 + side][shift : shift + earlier[2 * j].shape[0]] = earlier[2 * j + side][...]
        shift += earlier[2 * j].shape[0]

    def one_head(i, _):
        place = base + i
        here = columns(order, place, size)
        mine = own_aux[place]
        queries, grads, delta = query[:, here], grad[:, here], mine[1:2, :rows]
        norms = [mine[0:1, :rows] + (mine[2:3, j : j + 1] if j else 0.0) for j in range(3)]
        if both:
            extra = other[start + i, 2 * rows :].astype(jnp.float32)
            theirs = jnp.concatenate(
                [
                    extra[0:2] + extra[4:6] + extra[8:10],
                    (extra[2:4] + extra[6:8] + extra[10:12])[:, : rows - size],
                ],
                axis=1,
            )
            norms = [
                jnp.concatenate([norms[j], theirs[0:1] + extra[12:13, j : j + 1]], axis=1) for j in range(3)
            ]
            queries = jnp.concatenate([queries, other[start + i, :rows]], axis=0)
            grads = jnp.concatenate([grads, other[start + i, rows : 2 * rows]], axis=0)
            delta = jnp.concatenate([delta, theirs[1:2]], axis=1)
        keys = jnp.concatenate([key[:, here], lower[near + i, 0], upper[near + i, 0]], axis=0)
        values = jnp.concatenate([value[:, here], lower[near + i, 1], upper[near + i, 1]], axis=0)
        norm = jnp.concatenate([jnp.broadcast_to(row, (rows, row.shape[1])) for row in norms], axis=0)
        weights = jnp.exp2(dot(keys, queries, NT) * (score_scale * LOG2E) - norm)
        value_terms = dot(weights.astype(jnp.bfloat16), grads).astype(jnp.bfloat16)
        grad_scores = (weights * (dot(values, grads, NT) - delta)).astype(jnp.bfloat16)
        key_terms = (dot(grad_scores, queries) * score_scale).astype(jnp.bfloat16)
        query_terms = (dot(grad_scores, keys, TN) * score_scale).astype(jnp.bfloat16)
        own_query[i] = query_terms[:rows]
        if both:
            other_query[i] = query_terms[rows:]
        for j in range(3):
            to = i + shift if j else i
            refs[j][to, 0] = key_terms[j * rows : (j + 1) * rows]
            refs[j][to, 1] = value_terms[j * rows : (j + 1) * rows]
        return 0

    lax.fori_loop(0, count, one_head, 0)


def terms(order, own_aux, query, grad, other, key, value, lower, upper, base, count, start=0, near=0, earlier=(), cost=1):
    rows, features = query.shape
    size = features // own_aux.shape[0]
    both = other is not None
    pair = jax.ShapeDtypeStruct((count, 2, rows, size), jnp.bfloat16)
    total = count + sum(low.shape[0] for low, _ in earlier)
    side = jax.ShapeDtypeStruct((total, 2, rows, size), jnp.bfloat16)
    single = jax.ShapeDtypeStruct((count, rows, size), jnp.bfloat16)
    return kernel_call(
        functools.partial(terms_kernel, base=base, start=start, near=near, both=both, kept=len(earlier), score_scale=1.0 / math.sqrt(size)),
        "terms",
        [SCALAR] + [WHOLE] * (7 + both + 2 * len(earlier)),
        [WHOLE] * (4 + both),
        [single] * (1 + both) + [pair, side, side],
        cost=cost,
    )(order, own_aux, query, grad, *[other] * both, key, value, lower, upper, *(x for two in earlier for x in two))


def finish_query_kernel(order, *refs, plan):
    result = refs[-1]
    size = refs[0].shape[2]
    for base, count, own, back in plan:

        def one_head(i, _, base=base, own=own, back=back):
            total = refs[own][i]
            if back is not None:
                total = (total.astype(jnp.float32) + refs[back][i].astype(jnp.float32)).astype(jnp.bfloat16)
            result[:, columns(order, base + i, size)] = total
            return 0

        lax.fori_loop(0, count, one_head, 0)


def finish_pair_kernel(order, *refs, plan):
    size = refs[0].shape[3]
    for base, count, own, lower, upper, shift in plan:

        def one_head(i, _, base=base, own=own, lower=lower, upper=upper, shift=shift):
            here = columns(order, base + i, size)
            for k, result in enumerate(refs[-2:]):
                total = (
                    refs[own][i, k].astype(jnp.float32)
                    + refs[lower][i + shift, k].astype(jnp.float32)
                    + refs[upper][i + shift, k].astype(jnp.float32)
                )
                result[:, here] = total.astype(jnp.bfloat16)
            return 0

        lax.fori_loop(0, count, one_head, 0)


def finish(kernel, order, operands, plan, rows, features, count, **more):
    return kernel_call(
        functools.partial(kernel, plan=tuple(plan)),
        "finish",
        [SCALAR] + [WHOLE] * len(operands),
        [WHOLE] * count,
        [jax.ShapeDtypeStruct((rows, features), jnp.bfloat16)] * count,
        **more,
    )(order, *operands)


def mark_kernel(*refs):
    refs[-1][...] = jnp.zeros(refs[-1].shape, jnp.float32)


def mark(*values):
    return kernel_call(
        mark_kernel,
        "mark",
        [ANY] * len(values),
        WHOLE,
        jax.ShapeDtypeStruct((8, 128), jnp.float32),
        cost=LONG,
        effects=True,
    )(*values)


def after(value, other):
    return lax.optimization_barrier((value, other))[0]


def split(count):
    first = count - count // 2 + 0
    return (first, count - first) if count > first else (first,)


def exchange(count, window, log_norm, query, grad, out, key, value):
    rows, features = query.shape
    heads = log_norm.shape[0]
    tiles = lax.axis_size("tile")
    beside = [(i, (i + tiles // 2) % tiles) for i in range(tiles)]
    up = [(i, i + 1) for i in range(tiles - 1) if (i + 1) % GRID_WIDTH]
    down = [(b, a) for a, b in up]
    move = lambda value, pairs: lax.ppermute(value, "tile", pairs)
    sizes = split(count)
    first, first_pair, order = first_pack(
        window, log_norm, query, grad, out, key, value, sizes[0], count
    )
    *later, own_aux, pair = pack(order, window, log_norm, query, grad, out, key, value, sizes[1:], sizes[0])
    first_sides = move(first_pair, up), move(first_pair, down)
    sides = move(pair, up), move(pair, down)
    others = [move(first, beside)]
    for send in later:
        others.append(move(after(send, others[0]), beside))
    jobs = [(sum(sizes[:c]), size, other, c > 0 or count == heads) for c, (size, other) in enumerate(zip(sizes, others))]
    if count < heads:
        jobs.insert(1, (count, heads - count, None, True))
    query_parts, query_plan, pair_parts, pair_plan, waiting, held = [], [], [], [], [], []

    def add(operands, operand):
        operands.append(operand)
        return len(operands) - 1

    below = above = None
    later_order = order
    own_query = order
    for base, size, other, send in jobs:
        own_query, *made = terms(
            after(order, mark(other) if base == 0 else own_query),
            own_aux,
            query,
            grad,
            other,
            key,
            value,
            *(sides if base and other is not None else first_sides),
            base,
            size,
            near=sizes[0] if other is None else 0,
            earlier=waiting if send else (),
            cost=LONG if other is not None and base else 1,
        )
        back = None if other is None else add(query_parts, move(after(made.pop(0), others[-1]), beside))
        query_plan.append((base, size, add(query_parts, own_query), back))
        held.append((base, size, add(pair_parts, made[0])))
        waiting.append((made[1], made[2]))
        if send:
            sent = (made[2], made[1])
            if below is not None:
                later_order = after(order, mark(query_parts[0], below, above))
            below, above = move(sent[0], up), move(sent[1], down)
            places = add(pair_parts, below), add(pair_parts, above)
            shift = 0
            for entry in held:
                pair_plan.append((*entry, *places, shift))
                shift += entry[1]
            waiting, held = [], []
    (grad_query,) = finish(
        finish_query_kernel, later_order, query_parts, query_plan, rows, features, 1, cost=LONG
    )
    pair_parts = after(pair_parts, grad_query)
    return grad_query, *finish(finish_pair_kernel, order, pair_parts, pair_plan, rows, features, 2)


def body(query_tokens, key_tokens, value_tokens, forward_out, out_grad, log_norm, window_ids):
    window = window_ids[:, 0, :]
    heads = log_norm.shape[0]
    least = max(heads - SPARED, 1)
    count = jnp.sum((window[:, 0] >= 0).astype(jnp.int32))
    return lax.switch(
        jnp.maximum(count - least, 0),
        [functools.partial(exchange, n) for n in range(least, heads + 1)],
        window,
        log_norm,
        query_tokens,
        out_grad,
        forward_out,
        key_tokens,
        value_tokens,
    )


def solution(mesh):
    placed = (
        P(("group", "tile"), None),
        P(("group", "tile"), None),
        P(("group", "tile"), None),
        P(("group", "tile"), None),
        P(("group", "tile"), None),
        P(None, ("group", "tile")),
        P(None, "tile", None),
    )
    return jax.shard_map(
        body,
        mesh=mesh,
        in_specs=placed,
        out_specs=(
            P(("group", "tile"), None),
            P(("group", "tile"), None),
            P(("group", "tile"), None),
        ),
        check_vma=False,
    )
```

```python
import functools
import math

import jax
import jax.numpy as jnp
from jax import lax
from jax.experimental import pallas as pl
from jax.experimental.pallas import tpu as pltpu
from jax.sharding import PartitionSpec as P

GRID_WIDTH = 8
ABSENT = 1e30
LOG2E = 1.4426950408889634
NT = (((1,), (1,)), ((), ()))
TN = (((0,), (0,)), ((), ()))
VMEM_LIMIT = 24 * 2**20
EXTRA = 16
SPARED = 4
LONG = 3 * 10**10


def dot(a, b, dims=(((1,), (0,)), ((), ()))):
    return lax.dot_general(a, b, dims, preferred_element_type=jnp.float32)


def short(value):
    return value.astype(jnp.bfloat16).astype(jnp.float32)


WHOLE = pl.BlockSpec(memory_space=pltpu.VMEM)
SCALAR = pl.BlockSpec(memory_space=pltpu.SMEM)
ANY = pl.BlockSpec(memory_space=pl.ANY)


def kernel_call(kernel, name, in_specs, out_specs, out_shape, cost=1, effects=False, **more):
    return pl.pallas_call(
        kernel,
        out_shape=out_shape,
        in_specs=in_specs,
        out_specs=out_specs,
        compiler_params=pltpu.CompilerParams(vmem_limit_bytes=VMEM_LIMIT, has_side_effects=effects),
        cost_estimate=pl.CostEstimate(flops=cost, bytes_accessed=1, transcendentals=0),
        name=name,
        **more,
    )


def columns(order, place, size):
    return pl.ds(pl.multiple_of(order[place] * size, size), size)


def write_order(window, order):
    heads = window.shape[1]
    on = [(window[0, h] >= 0).astype(jnp.int32) for h in range(heads)]
    first, last = jnp.int32(0), sum(on)
    for h in range(heads):
        order[jnp.where(on[h] > 0, first, last)] = jnp.int32(h)
        first, last = first + on[h], last + 1 - on[h]


def flag_row(window, head, slots, lane):
    row = jnp.zeros(lane.shape, jnp.float32)
    for place, slot in slots:
        row = jnp.where(lane == place, jnp.where(window[slot, head] < 0, ABSENT, 0.0), row)
    return row


def describe(log_norm, grad, out, head, here, ones):
    product = grad[:, here].astype(jnp.float32) * out[:, here].astype(jnp.float32)
    high = short(product)
    both = jnp.concatenate([high.astype(jnp.bfloat16), (product - high).astype(jnp.bfloat16)], axis=1)
    return log_norm[pl.ds(head, 1), :] * LOG2E, dot(ones, both, NT)[0:1]


def fill(chunk, i, window, query, grad, head, here, lines, rows32, lane):
    rows, size = query.shape[0], chunk.shape[2]
    chunk[i, :rows] = query[:, here]
    chunk[i, rows : 2 * rows] = grad[:, here]
    one = short(lines)
    two = short(lines - one)
    for k, part in enumerate((one, two, lines - one - two)):
        rows32[4 * k : 4 * k + 2, :] = part[:, :size]
        rows32[4 * k + 2 : 4 * k + 4, : rows - size] = part[:, size:]
    rows32[12:13, :] = flag_row(window, head, ((0, 0), (1, 3), (2, 4)), lane)
    chunk[i, 2 * rows :] = rows32[...].astype(jnp.bfloat16)


def fill_pair(pair, order, key, value, base, count, to):
    size = pair.shape[3]

    def one_head(i, _):
        here = columns(order, base + i, size)
        pair[to + i, 0], pair[to + i, 1] = key[:, here], value[:, here]
        return 0

    lax.fori_loop(0, count, one_head, 0)


def first_pack_kernel(window, log_norm, query, grad, out, key, value, chunk, pair, order, rows32, *, sent):
    heads = log_norm.shape[0]
    size = query.shape[1] // heads
    write_order(window, order)
    rows32[...] = jnp.zeros(rows32.shape, jnp.float32)
    ones = jnp.ones((8, 2 * size), jnp.bfloat16)
    lane = lax.broadcasted_iota(jnp.int32, (1, size), 1)

    def one_head(i, _):
        head, here = order[i], columns(order, i, size)
        lines = jnp.concatenate(describe(log_norm, grad, out, head, here, ones), axis=0)
        fill(chunk, i, window, query, grad, head, here, lines, rows32, lane)
        return 0

    lax.fori_loop(0, chunk.shape[0], one_head, 0, unroll=True)
    fill_pair(pair, order, key, value, 0, chunk.shape[0], 0)
    fill_pair(pair, order, key, value, sent, heads - sent, chunk.shape[0])


def first_pack(window, log_norm, query, grad, out, key, value, count, sent):
    heads, rows = log_norm.shape
    size = query.shape[1] // heads
    return kernel_call(
        functools.partial(first_pack_kernel, sent=sent),
        "first_pack",
        [SCALAR] + [WHOLE] * 6,
        [WHOLE, WHOLE, SCALAR],
        [
            jax.ShapeDtypeStruct((count, 2 * rows + EXTRA, size), jnp.bfloat16),
            jax.ShapeDtypeStruct((count + heads - sent, 2, rows, size), jnp.bfloat16),
            jax.ShapeDtypeStruct((heads,), jnp.int32),
        ],
        scratch_shapes=[pltpu.VMEM((EXTRA, size), jnp.float32)],
    )(window, log_norm, query, grad, out, key, value)


def pack_kernel(order, window, log_norm, query, grad, out, key, value, *refs, sizes, base):
    chunks, (own_aux, pair, rows32) = refs[: len(sizes)], refs[len(sizes) :]
    heads, rows = log_norm.shape
    size = query.shape[1] // heads
    rows32[...] = jnp.zeros(rows32.shape, jnp.float32)
    ones = jnp.ones((8, 2 * size), jnp.bfloat16)
    lane = lax.broadcasted_iota(jnp.int32, (1, size), 1)

    def one_head(place, _):
        head, here = order[place], columns(order, place, size)
        norm, delta = describe(log_norm, grad, out, head, here, ones)
        own_aux[place, 0:1, :rows] = norm
        own_aux[place, 1:2, :rows] = delta
        own_aux[place, 2:3, :size] = flag_row(window, head, ((1, 1), (2, 2)), lane)
        return 0

    lax.fori_loop(0, heads, one_head, 0, unroll=3)
    fill_pair(pair, order, key, value, base, sum(sizes), 0)
    for chunk, count in zip(chunks, sizes):

        def one_send(i, _, chunk=chunk, base=base):
            head, here = order[base + i], columns(order, base + i, size)
            lines = own_aux[base + i, 0:2, :rows]
            fill(chunk, i, window, query, grad, head, here, lines, rows32, lane)
            return 0

        lax.fori_loop(0, count, one_send, 0)
        base += count


def pack(order, window, log_norm, query, grad, out, key, value, sizes, base):
    heads, rows = log_norm.shape
    features = query.shape[1]
    size = features // heads
    lanes = -(-rows // 128) * 128
    bf16 = jnp.bfloat16
    return kernel_call(
        functools.partial(pack_kernel, sizes=sizes, base=base),
        "pack",
        [SCALAR] * 2 + [WHOLE] * 6,
        [WHOLE] * (len(sizes) + 2),
        [jax.ShapeDtypeStruct((n, 2 * rows + EXTRA, size), bf16) for n in sizes]
        + [
            jax.ShapeDtypeStruct((heads, 4, lanes), jnp.float32),
            jax.ShapeDtypeStruct((sum(sizes), 2, rows, size), bf16),
        ],
        scratch_shapes=[pltpu.VMEM((EXTRA, size), jnp.float32)],
    )(order, window, log_norm, query, grad, out, key, value)


def terms_kernel(order, own_aux, query, grad, *refs, base, start, near, both, kept, score_scale):
    rows = query.shape[0]
    refs = list(refs)
    other = refs.pop(0) if both else None
    key, value, lower, upper = refs[:4]
    earlier, refs = refs[4 : 4 + 2 * kept], refs[4 + 2 * kept :]
    own_query = refs.pop(0)
    other_query = refs.pop(0) if both else None
    count, _, _, size = refs[0].shape
    shift = 0
    for j in range(kept):
        for side in range(2):
            refs[1 + side][shift : shift + earlier[2 * j].shape[0]] = earlier[2 * j + side][...]
        shift += earlier[2 * j].shape[0]

    def one_head(i, _):
        place = base + i
        here = columns(order, place, size)
        mine = own_aux[place]
        queries, grads, delta = query[:, here], grad[:, here], mine[1:2, :rows]
        norms = [mine[0:1, :rows] + (mine[2:3, j : j + 1] if j else 0.0) for j in range(3)]
        if both:
            extra = other[start + i, 2 * rows :].astype(jnp.float32)
            theirs = jnp.concatenate(
                [
                    extra[0:2] + extra[4:6] + extra[8:10],
                    (extra[2:4] + extra[6:8] + extra[10:12])[:, : rows - size],
                ],
                axis=1,
            )
            norms = [
                jnp.concatenate([norms[j], theirs[0:1] + extra[12:13, j : j + 1]], axis=1) for j in range(3)
            ]
            queries = jnp.concatenate([queries, other[start + i, :rows]], axis=0)
            grads = jnp.concatenate([grads, other[start + i, rows : 2 * rows]], axis=0)
            delta = jnp.concatenate([delta, theirs[1:2]], axis=1)
        keys = jnp.concatenate([key[:, here], lower[near + i, 0], upper[near + i, 0]], axis=0)
        values = jnp.concatenate([value[:, here], lower[near + i, 1], upper[near + i, 1]], axis=0)
        norm = jnp.concatenate([jnp.broadcast_to(row, (rows, row.shape[1])) for row in norms], axis=0)
        weights = jnp.exp2(dot(keys, queries, NT) * (score_scale * LOG2E) - norm)
        value_terms = dot(weights.astype(jnp.bfloat16), grads).astype(jnp.bfloat16)
        grad_scores = (weights * (dot(values, grads, NT) - delta)).astype(jnp.bfloat16)
        key_terms = (dot(grad_scores, queries) * score_scale).astype(jnp.bfloat16)
        query_terms = (dot(grad_scores, keys, TN) * score_scale).astype(jnp.bfloat16)
        own_query[i] = query_terms[:rows]
        if both:
            other_query[i] = query_terms[rows:]
        for j in range(3):
            to = i + shift if j else i
            refs[j][to, 0] = key_terms[j * rows : (j + 1) * rows]
            refs[j][to, 1] = value_terms[j * rows : (j + 1) * rows]
        return 0

    lax.fori_loop(0, count, one_head, 0)


def terms(order, own_aux, query, grad, other, key, value, lower, upper, base, count, start=0, near=0, earlier=(), cost=1):
    rows, features = query.shape
    size = features // own_aux.shape[0]
    both = other is not None
    pair = jax.ShapeDtypeStruct((count, 2, rows, size), jnp.bfloat16)
    total = count + sum(low.shape[0] for low, _ in earlier)
    side = jax.ShapeDtypeStruct((total, 2, rows, size), jnp.bfloat16)
    single = jax.ShapeDtypeStruct((count, rows, size), jnp.bfloat16)
    return kernel_call(
        functools.partial(terms_kernel, base=base, start=start, near=near, both=both, kept=len(earlier), score_scale=1.0 / math.sqrt(size)),
        "terms",
        [SCALAR] + [WHOLE] * (7 + both + 2 * len(earlier)),
        [WHOLE] * (4 + both),
        [single] * (1 + both) + [pair, side, side],
        cost=cost,
    )(order, own_aux, query, grad, *[other] * both, key, value, lower, upper, *(x for two in earlier for x in two))


def finish_query_kernel(order, *refs, plan):
    result = refs[-1]
    size = refs[0].shape[2]
    for base, count, own, back in plan:

        def one_head(i, _, base=base, own=own, back=back):
            total = refs[own][i]
            if back is not None:
                total = (total.astype(jnp.float32) + refs[back][i].astype(jnp.float32)).astype(jnp.bfloat16)
            result[:, columns(order, base + i, size)] = total
            return 0

        lax.fori_loop(0, count, one_head, 0, unroll=True)


def finish_pair_kernel(order, *refs, plan):
    size = refs[0].shape[3]
    for base, count, own, lower, upper, shift in plan:

        def one_head(i, _, base=base, own=own, lower=lower, upper=upper, shift=shift):
            here = columns(order, base + i, size)
            for k, result in enumerate(refs[-2:]):
                total = (
                    refs[own][i, k].astype(jnp.float32)
                    + refs[lower][i + shift, k].astype(jnp.float32)
                    + refs[upper][i + shift, k].astype(jnp.float32)
                )
                result[:, here] = total.astype(jnp.bfloat16)
            return 0

        lax.fori_loop(0, count, one_head, 0, unroll=True)


def finish(kernel, order, operands, plan, rows, features, count, **more):
    return kernel_call(
        functools.partial(kernel, plan=tuple(plan)),
        "finish",
        [SCALAR] + [WHOLE] * len(operands),
        [WHOLE] * count,
        [jax.ShapeDtypeStruct((rows, features), jnp.bfloat16)] * count,
        **more,
    )(order, *operands)


def mark_kernel(*refs):
    refs[-1][...] = jnp.zeros(refs[-1].shape, jnp.float32)


def mark(*values):
    return kernel_call(
        mark_kernel,
        "mark",
        [ANY] * len(values),
        WHOLE,
        jax.ShapeDtypeStruct((8, 128), jnp.float32),
        cost=LONG,
        effects=True,
    )(*values)


def after(value, other):
    return lax.optimization_barrier((value, other))[0]


def split(count):
    first = count - count // 2 + 0
    return (first, count - first) if count > first else (first,)


def exchange(count, window, log_norm, query, grad, out, key, value):
    rows, features = query.shape
    heads = log_norm.shape[0]
    tiles = lax.axis_size("tile")
    beside = [(i, (i + tiles // 2) % tiles) for i in range(tiles)]
    up = [(i, i + 1) for i in range(tiles - 1) if (i + 1) % GRID_WIDTH]
    down = [(b, a) for a, b in up]
    move = lambda value, pairs: lax.ppermute(value, "tile", pairs)
    sizes = split(count)
    first, first_pair, order = first_pack(
        window, log_norm, query, grad, out, key, value, sizes[0], count
    )
    *later, own_aux, pair = pack(order, window, log_norm, query, grad, out, key, value, sizes[1:], sizes[0])
    first_sides = move(first_pair, up), move(first_pair, down)
    sides = move(pair, up), move(pair, down)
    others = [move(first, beside)]
    for send in later:
        others.append(move(after(send, others[0]), beside))
    jobs = [(sum(sizes[:c]), size, other, c > 0 or count == heads) for c, (size, other) in enumerate(zip(sizes, others))]
    if count < heads:
        jobs.insert(1, (count, heads - count, None, True))
    query_parts, query_plan, pair_parts, pair_plan, waiting, held = [], [], [], [], [], []

    def add(operands, operand):
        operands.append(operand)
        return len(operands) - 1

    below = above = None
    later_order = order
    own_query = order
    for base, size, other, send in jobs:
        own_query, *made = terms(
            after(order, mark(other) if base == 0 else own_query),
            own_aux,
            query,
            grad,
            other,
            key,
            value,
            *(sides if base and other is not None else first_sides),
            base,
            size,
            near=sizes[0] if other is None else 0,
            earlier=waiting if send else (),
            cost=LONG if other is not None and base else 1,
        )
        back = None if other is None else add(query_parts, move(after(made.pop(0), others[-1]), beside))
        query_plan.append((base, size, add(query_parts, own_query), back))
        held.append((base, size, add(pair_parts, made[0])))
        waiting.append((made[1], made[2]))
        if send:
            sent = (made[2], made[1])
            if below is not None:
                if heads - count == 2:
                    sent = after(sent, (below, above))
                else:
                    later_order = after(order, mark(query_parts[0], below, above))
            below, above = move(sent[0], up), move(sent[1], down)
            places = add(pair_parts, below), add(pair_parts, above)
            shift = 0
            for entry in held:
                pair_plan.append((*entry, *places, shift))
                shift += entry[1]
            waiting, held = [], []
    (grad_query,) = finish(
        finish_query_kernel, later_order, query_parts, query_plan, rows, features, 1, cost=LONG
    )
    pair_parts = after(pair_parts, grad_query)
    return grad_query, *finish(finish_pair_kernel, order, pair_parts, pair_plan, rows, features, 2)


def body(query_tokens, key_tokens, value_tokens, forward_out, out_grad, log_norm, window_ids):
    window = window_ids.transpose(2, 1, 0)[:, 0, :]
    heads = log_norm.shape[0]
    least = max(heads - SPARED, 1)
    count = jnp.sum((window[0] >= 0).astype(jnp.int32))
    return lax.switch(
        jnp.maximum(count - least, 0),
        [functools.partial(exchange, n) for n in range(least, heads + 1)],
        window,
        log_norm,
        query_tokens,
        out_grad,
        forward_out,
        key_tokens,
        value_tokens,
    )


def solution(mesh):
    placed = (
        P(("group", "tile"), None),
        P(("group", "tile"), None),
        P(("group", "tile"), None),
        P(("group", "tile"), None),
        P(("group", "tile"), None),
        P(None, ("group", "tile")),
        P(None, "tile", None),
    )
    return jax.shard_map(
        body,
        mesh=mesh,
        in_specs=placed,
        out_specs=(
            P(("group", "tile"), None),
            P(("group", "tile"), None),
            P(("group", "tile"), None),
        ),
        check_vma=False,
    )
```

```python
import functools
import math

import jax
import jax.numpy as jnp
from jax import lax
from jax.experimental import pallas as pl
from jax.experimental.pallas import tpu as pltpu
from jax.sharding import PartitionSpec as P

GRID_WIDTH = 8
ABSENT = 1e30
LOG2E = 1.4426950408889634
NT = (((1,), (1,)), ((), ()))
TN = (((0,), (0,)), ((), ()))
VMEM_LIMIT = 24 * 2**20
EXTRA = 16
SPARED = 4
LONG = 3 * 10**10


def dot(a, b, dims=(((1,), (0,)), ((), ()))):
    return lax.dot_general(a, b, dims, preferred_element_type=jnp.float32)


def short(value):
    return value.astype(jnp.bfloat16).astype(jnp.float32)


WHOLE = pl.BlockSpec(memory_space=pltpu.VMEM)
SCALAR = pl.BlockSpec(memory_space=pltpu.SMEM)
ANY = pl.BlockSpec(memory_space=pl.ANY)


def kernel_call(kernel, name, in_specs, out_specs, out_shape, cost=1, effects=False, **more):
    return pl.pallas_call(
        kernel,
        out_shape=out_shape,
        in_specs=in_specs,
        out_specs=out_specs,
        compiler_params=pltpu.CompilerParams(vmem_limit_bytes=VMEM_LIMIT, has_side_effects=effects),
        cost_estimate=pl.CostEstimate(flops=cost, bytes_accessed=1, transcendentals=0),
        name=name,
        **more,
    )


def columns(order, place, size):
    return pl.ds(pl.multiple_of(order[place] * size, size), size)


def write_order(window, order):
    heads = window.shape[1]
    on = [(window[0, h] >= 0).astype(jnp.int32) for h in range(heads)]
    first, last = jnp.int32(0), sum(on)
    for h in range(heads):
        order[jnp.where(on[h] > 0, first, last)] = jnp.int32(h)
        first, last = first + on[h], last + 1 - on[h]


def flag_row(window, head, slots, lane):
    row = jnp.zeros(lane.shape, jnp.float32)
    for place, slot in slots:
        row = jnp.where(lane == place, jnp.where(window[slot, head] < 0, ABSENT, 0.0), row)
    return row


def describe(log_norm, grad, out, head, here, ones):
    product = grad[:, here].astype(jnp.float32) * out[:, here].astype(jnp.float32)
    high = short(product)
    both = jnp.concatenate([high.astype(jnp.bfloat16), (product - high).astype(jnp.bfloat16)], axis=1)
    return log_norm[pl.ds(head, 1), :] * LOG2E, dot(ones, both, NT)[0:1]


def fill(chunk, i, window, query, grad, head, here, lines, rows32, lane):
    rows, size = query.shape[0], chunk.shape[2]
    chunk[i, :rows] = query[:, here]
    chunk[i, rows : 2 * rows] = grad[:, here]
    one = short(lines)
    two = short(lines - one)
    for k, part in enumerate((one, two, lines - one - two)):
        rows32[4 * k : 4 * k + 2, :] = part[:, :size]
        rows32[4 * k + 2 : 4 * k + 4, : rows - size] = part[:, size:]
    rows32[12:13, :] = flag_row(window, head, ((0, 0), (1, 3), (2, 4)), lane)
    chunk[i, 2 * rows :] = rows32[...].astype(jnp.bfloat16)


def fill_pair(pair, order, key, value, base, count, to):
    size = pair.shape[3]

    def one_head(i, _):
        here = columns(order, base + i, size)
        pair[to + i, 0], pair[to + i, 1] = key[:, here], value[:, here]
        return 0

    lax.fori_loop(0, count, one_head, 0)


def first_pack_kernel(window, log_norm, query, grad, out, key, value, chunk, pair, order, rows32, *, sent):
    heads = log_norm.shape[0]
    size = query.shape[1] // heads
    write_order(window, order)
    rows32[...] = jnp.zeros(rows32.shape, jnp.float32)
    ones = jnp.ones((8, 2 * size), jnp.bfloat16)
    lane = lax.broadcasted_iota(jnp.int32, (1, size), 1)

    def one_head(i, _):
        head, here = order[i], columns(order, i, size)
        lines = jnp.concatenate(describe(log_norm, grad, out, head, here, ones), axis=0)
        fill(chunk, i, window, query, grad, head, here, lines, rows32, lane)
        return 0

    lax.fori_loop(0, chunk.shape[0], one_head, 0, unroll=True)
    fill_pair(pair, order, key, value, 0, chunk.shape[0], 0)
    fill_pair(pair, order, key, value, sent, heads - sent, chunk.shape[0])


def first_pack(window, log_norm, query, grad, out, key, value, count, sent):
    heads, rows = log_norm.shape
    size = query.shape[1] // heads
    return kernel_call(
        functools.partial(first_pack_kernel, sent=sent),
        "first_pack",
        [SCALAR] + [WHOLE] * 6,
        [WHOLE, WHOLE, SCALAR],
        [
            jax.ShapeDtypeStruct((count, 2 * rows + EXTRA, size), jnp.bfloat16),
            jax.ShapeDtypeStruct((count + heads - sent, 2, rows, size), jnp.bfloat16),
            jax.ShapeDtypeStruct((heads,), jnp.int32),
        ],
        scratch_shapes=[pltpu.VMEM((EXTRA, size), jnp.float32)],
    )(window, log_norm, query, grad, out, key, value)


def pack_kernel(order, window, log_norm, query, grad, out, key, value, *refs, sizes, base):
    chunks, (own_aux, pair, rows32) = refs[: len(sizes)], refs[len(sizes) :]
    heads, rows = log_norm.shape
    size = query.shape[1] // heads
    rows32[...] = jnp.zeros(rows32.shape, jnp.float32)
    ones = jnp.ones((8, 2 * size), jnp.bfloat16)
    lane = lax.broadcasted_iota(jnp.int32, (1, size), 1)

    def one_head(place, _):
        head, here = order[place], columns(order, place, size)
        norm, delta = describe(log_norm, grad, out, head, here, ones)
        own_aux[place, 0:1, :rows] = norm
        own_aux[place, 1:2, :rows] = delta
        own_aux[place, 2:3, :size] = flag_row(window, head, ((1, 1), (2, 2)), lane)
        return 0

    lax.fori_loop(0, heads, one_head, 0, unroll=3)
    fill_pair(pair, order, key, value, base, sum(sizes), 0)
    for chunk, count in zip(chunks, sizes):

        def one_send(i, _, chunk=chunk, base=base):
            head, here = order[base + i], columns(order, base + i, size)
            lines = own_aux[base + i, 0:2, :rows]
            fill(chunk, i, window, query, grad, head, here, lines, rows32, lane)
            return 0

        lax.fori_loop(0, count, one_send, 0)
        base += count


def pack(order, window, log_norm, query, grad, out, key, value, sizes, base):
    heads, rows = log_norm.shape
    features = query.shape[1]
    size = features // heads
    lanes = -(-rows // 128) * 128
    bf16 = jnp.bfloat16
    return kernel_call(
        functools.partial(pack_kernel, sizes=sizes, base=base),
        "pack",
        [SCALAR] * 2 + [WHOLE] * 6,
        [WHOLE] * (len(sizes) + 2),
        [jax.ShapeDtypeStruct((n, 2 * rows + EXTRA, size), bf16) for n in sizes]
        + [
            jax.ShapeDtypeStruct((heads, 4, lanes), jnp.float32),
            jax.ShapeDtypeStruct((sum(sizes), 2, rows, size), bf16),
        ],
        scratch_shapes=[pltpu.VMEM((EXTRA, size), jnp.float32)],
    )(order, window, log_norm, query, grad, out, key, value)


def terms_kernel(order, own_aux, query, grad, *refs, base, start, near, both, kept, score_scale):
    rows = query.shape[0]
    refs = list(refs)
    other = refs.pop(0) if both else None
    key, value, lower, upper = refs[:4]
    earlier, refs = refs[4 : 4 + 2 * kept], refs[4 + 2 * kept :]
    own_query = refs.pop(0)
    other_query = refs.pop(0) if both else None
    count, _, _, size = refs[0].shape
    shift = 0
    for j in range(kept):
        for side in range(2):
            refs[1 + side][shift : shift + earlier[2 * j].shape[0]] = earlier[2 * j + side][...]
        shift += earlier[2 * j].shape[0]

    def one_head(i, _):
        place = base + i
        here = columns(order, place, size)
        mine = own_aux[place]
        queries, grads, delta = query[:, here], grad[:, here], mine[1:2, :rows]
        norms = [mine[0:1, :rows] + (mine[2:3, j : j + 1] if j else 0.0) for j in range(3)]
        if both:
            extra = other[start + i, 2 * rows :].astype(jnp.float32)
            theirs = jnp.concatenate(
                [
                    extra[0:2] + extra[4:6] + extra[8:10],
                    (extra[2:4] + extra[6:8] + extra[10:12])[:, : rows - size],
                ],
                axis=1,
            )
            norms = [
                jnp.concatenate([norms[j], theirs[0:1] + extra[12:13, j : j + 1]], axis=1) for j in range(3)
            ]
            queries = jnp.concatenate([queries, other[start + i, :rows]], axis=0)
            grads = jnp.concatenate([grads, other[start + i, rows : 2 * rows]], axis=0)
            delta = jnp.concatenate([delta, theirs[1:2]], axis=1)
        keys = jnp.concatenate([key[:, here], lower[near + i, 0], upper[near + i, 0]], axis=0)
        values = jnp.concatenate([value[:, here], lower[near + i, 1], upper[near + i, 1]], axis=0)
        norm = jnp.concatenate([jnp.broadcast_to(row, (rows, row.shape[1])) for row in norms], axis=0)
        weights = jnp.exp2(dot(keys, queries, NT) * (score_scale * LOG2E) - norm)
        value_terms = dot(weights.astype(jnp.bfloat16), grads).astype(jnp.bfloat16)
        grad_scores = (weights * (dot(values, grads, NT) - delta)).astype(jnp.bfloat16)
        key_terms = (dot(grad_scores, queries) * score_scale).astype(jnp.bfloat16)
        query_terms = (dot(grad_scores, keys, TN) * score_scale).astype(jnp.bfloat16)
        own_query[i] = query_terms[:rows]
        if both:
            other_query[i] = query_terms[rows:]
        for j in range(3):
            to = i + shift if j else i
            refs[j][to, 0] = key_terms[j * rows : (j + 1) * rows]
            refs[j][to, 1] = value_terms[j * rows : (j + 1) * rows]
        return 0

    lax.fori_loop(0, count, one_head, 0)


def terms(order, own_aux, query, grad, other, key, value, lower, upper, base, count, start=0, near=0, earlier=(), cost=1):
    rows, features = query.shape
    size = features // own_aux.shape[0]
    both = other is not None
    pair = jax.ShapeDtypeStruct((count, 2, rows, size), jnp.bfloat16)
    total = count + sum(low.shape[0] for low, _ in earlier)
    side = jax.ShapeDtypeStruct((total, 2, rows, size), jnp.bfloat16)
    single = jax.ShapeDtypeStruct((count, rows, size), jnp.bfloat16)
    return kernel_call(
        functools.partial(terms_kernel, base=base, start=start, near=near, both=both, kept=len(earlier), score_scale=1.0 / math.sqrt(size)),
        "terms",
        [SCALAR] + [WHOLE] * (7 + both + 2 * len(earlier)),
        [WHOLE] * (4 + both),
        [single] * (1 + both) + [pair, side, side],
        cost=cost,
    )(order, own_aux, query, grad, *[other] * both, key, value, lower, upper, *(x for two in earlier for x in two))


def finish_query_kernel(order, *refs, plan):
    result = refs[-1]
    size = refs[0].shape[2]
    for base, count, own, back in plan:

        def one_head(i, _, base=base, own=own, back=back):
            total = refs[own][i]
            if back is not None:
                total = (total.astype(jnp.float32) + refs[back][i].astype(jnp.float32)).astype(jnp.bfloat16)
            result[:, columns(order, base + i, size)] = total
            return 0

        lax.fori_loop(0, count, one_head, 0, unroll=True)


def finish_pair_kernel(order, *refs, plan):
    size = refs[0].shape[3]
    for base, count, own, lower, upper, shift in plan:

        def one_head(i, _, base=base, own=own, lower=lower, upper=upper, shift=shift):
            here = columns(order, base + i, size)
            for k, result in enumerate(refs[-2:]):
                total = (
                    refs[own][i, k].astype(jnp.float32)
                    + refs[lower][i + shift, k].astype(jnp.float32)
                    + refs[upper][i + shift, k].astype(jnp.float32)
                )
                result[:, here] = total.astype(jnp.bfloat16)
            return 0

        lax.fori_loop(0, count, one_head, 0, unroll=True)


def finish(kernel, order, operands, plan, rows, features, count, **more):
    return kernel_call(
        functools.partial(kernel, plan=tuple(plan)),
        "finish",
        [SCALAR] + [WHOLE] * len(operands),
        [WHOLE] * count,
        [jax.ShapeDtypeStruct((rows, features), jnp.bfloat16)] * count,
        **more,
    )(order, *operands)


def mark_kernel(*refs):
    refs[-1][...] = jnp.zeros(refs[-1].shape, jnp.float32)


def mark(*values):
    return kernel_call(
        mark_kernel,
        "mark",
        [ANY] * len(values),
        WHOLE,
        jax.ShapeDtypeStruct((8, 128), jnp.float32),
        cost=LONG,
        effects=True,
    )(*values)


def after(value, other):
    return lax.optimization_barrier((value, other))[0]


def split(count):
    first = count - count // 2 + 0
    return (first, count - first) if count > first else (first,)


def exchange(count, window, log_norm, query, grad, out, key, value):
    rows, features = query.shape
    heads = log_norm.shape[0]
    tiles = lax.axis_size("tile")
    beside = [(i, (i + tiles // 2) % tiles) for i in range(tiles)]
    up = [(i, i + 1) for i in range(tiles - 1) if (i + 1) % GRID_WIDTH]
    down = [(b, a) for a, b in up]
    move = lambda value, pairs: lax.ppermute(value, "tile", pairs)
    sizes = split(count)
    first, first_pair, order = first_pack(
        window, log_norm, query, grad, out, key, value, sizes[0], count
    )
    *later, own_aux, pair = pack(order, window, log_norm, query, grad, out, key, value, sizes[1:], sizes[0])
    first_sides = move(first_pair, up), move(first_pair, down)
    sides = move(pair, up), move(pair, down)
    others = [move(first, beside)]
    for send in later:
        others.append(move(after(send, others[0]), beside))
    jobs = [(sum(sizes[:c]), size, other, c > 0 or count == heads) for c, (size, other) in enumerate(zip(sizes, others))]
    if count < heads:
        jobs.insert(1, (count, heads - count, None, True))
    query_parts, query_plan, pair_parts, pair_plan, waiting, held = [], [], [], [], [], []

    def add(operands, operand):
        operands.append(operand)
        return len(operands) - 1

    below = above = None
    later_order = order
    own_query = order
    for base, size, other, send in jobs:
        own_query, *made = terms(
            after(order, mark(other) if base == 0 else own_query),
            own_aux,
            query,
            grad,
            other,
            key,
            value,
            *(sides if base and other is not None else first_sides),
            base,
            size,
            near=sizes[0] if other is None else 0,
            earlier=waiting if send else (),
            cost=LONG if other is not None and base else 1,
        )
        back = None if other is None else add(query_parts, move(after(made.pop(0), others[-1]), beside))
        query_plan.append((base, size, add(query_parts, own_query), back))
        held.append((base, size, add(pair_parts, made[0])))
        waiting.append((made[1], made[2]))
        if send:
            sent = (made[2], made[1])
            if below is not None:
                held_back = [query_parts[0]] if heads - count < 2 else []
                later_order = after(order, mark(*held_back, below, above))
            below, above = move(sent[0], up), move(sent[1], down)
            places = add(pair_parts, below), add(pair_parts, above)
            shift = 0
            for entry in held:
                pair_plan.append((*entry, *places, shift))
                shift += entry[1]
            waiting, held = [], []
    (grad_query,) = finish(
        finish_query_kernel, later_order, query_parts, query_plan, rows, features, 1, cost=LONG
    )
    pair_parts = after(pair_parts, grad_query)
    return grad_query, *finish(finish_pair_kernel, order, pair_parts, pair_plan, rows, features, 2)


def body(query_tokens, key_tokens, value_tokens, forward_out, out_grad, log_norm, window_ids):
    window = window_ids.transpose(2, 1, 0)[:, 0, :]
    heads = log_norm.shape[0]
    least = max(heads - SPARED, 1)
    count = jnp.sum((window[0] >= 0).astype(jnp.int32))
    return lax.switch(
        jnp.maximum(count - least, 0),
        [functools.partial(exchange, n) for n in range(least, heads + 1)],
        window,
        log_norm,
        query_tokens,
        out_grad,
        forward_out,
        key_tokens,
        value_tokens,
    )


def solution(mesh):
    placed = (
        P(("group", "tile"), None),
        P(("group", "tile"), None),
        P(("group", "tile"), None),
        P(("group", "tile"), None),
        P(("group", "tile"), None),
        P(None, ("group", "tile")),
        P(None, "tile", None),
    )
    return jax.shard_map(
        body,
        mesh=mesh,
        in_specs=placed,
        out_specs=(
            P(("group", "tile"), None),
            P(("group", "tile"), None),
            P(("group", "tile"), None),
        ),
        check_vma=False,
    )
```
